32 devices in a mesh: row: 8 (over z, core), col: 4 (over y, x).
Axes of the slice: x: 2, y: 2, z: 4, core: 2. Of those that a mesh axis runs over, the one named last changes fastest.
Arguments:
- source: bfloat16 [8192, 256], P(('row', 'col')), may hold values from -1.5 to 1.5
- target: bfloat16 [8192, 256], P(('col', 'row')), may hold values from -1.5 to 1.5
- g_init: float32 [8192], P('col'), may hold values from -25 to 25
- pairs: int32 [16, 16], P('row', 'col'), may hold values from 0 to 1, as said below
Outputs:
- f_out: float32 [8192], P('row')
- g_out: float32 [8192], P('col')
The draws below stay inside these ranges and needn't reach their ends.
Inputs may be any that keep to these rules, and one draw needn't show every extreme that they name: Values are 0 or 1; every block of source cells and every block of target cells has at least one kept pair; the share of kept pairs differs between devices' tiles.
All inputs are finite; a program needn't handle non-finite values.
Results may differ from the reference program's by a relative error of at most 0.0003.
Values may be sent and summed in bfloat16 or wider, within the bound.
A program may use at most 64 MiB of HBM per device.

```python
import jax
import jax.numpy as jnp
from jax import lax

DL = 256
BLK = 512
ROWS_DEV = 1024
COLS_DEV = 2048
NS = 8192
NT = 8192
NBR = 16
NBC = 16


cell_types = 8


trajectory_rank = 4


outlier_scale = 8.0


def atlas_cells(key, count, salt):
    shared = jax.random.fold_in(key, 7)
    centre_key, basis_key = jax.random.split(shared)
    root = jnp.sqrt(jnp.float32(DL))
    centres = 1.2247 * jax.random.normal(centre_key, (cell_types, DL), jnp.float32) / root
    basis = jax.random.normal(basis_key, (cell_types * trajectory_rank, DL), jnp.float32) / root
    own = jax.random.fold_in(key, salt)
    kind_key, place_key, noise_key, scale_key, odd_key, forced_key = jax.random.split(own, 6)
    kinds = jax.random.randint(kind_key, (count,), 0, cell_types)
    onehot = (kinds[:, None] == jnp.arange(cell_types, dtype=jnp.int32)[None, :]).astype(jnp.float32)
    place = 0.6 * jax.random.normal(place_key, (count, trajectory_rank), jnp.float32)
    mixing = (onehot[:, :, None] * place[:, None, :]).reshape(count, cell_types * trajectory_rank)
    noise = jax.random.normal(noise_key, (count, DL), jnp.float32) / root
    spread = jnp.exp(jax.random.uniform(scale_key, (count, 1), jnp.float32, jnp.log(jnp.float32(0.5)), jnp.log(jnp.float32(1.5))))
    forced = jax.random.randint(forced_key, (), 0, count)
    outlier = (jax.random.randint(odd_key, (count,), 0, 32) == 0) | (jnp.arange(count, dtype=jnp.int32) == forced)
    spread = jnp.where(outlier[:, None], jnp.float32(outlier_scale), spread)
    centre_part = jnp.dot(onehot, centres, precision=jax.lax.Precision.HIGHEST)
    trajectory = jnp.dot(mixing, basis, precision=jax.lax.Precision.HIGHEST)
    return jnp.clip(centre_part + trajectory + spread * noise, -1.5, 1.5)


def draw_source(key, part):
    return atlas_cells(key, NS, 21).astype(jnp.bfloat16)


def draw_target(key, part):
    return atlas_cells(key, NT, 22).astype(jnp.bfloat16)


def draw_g_init(key, part):
    first, second, third, fourth = jax.random.split(key, 4)
    marked = jax.random.randint(second, (NBC,), 0, 8) == 0
    chosen = jax.random.randint(fourth, (), 0, NBC)
    marked = marked | (jnp.arange(NBC, dtype=jnp.int32) == chosen)
    lift = jnp.repeat(marked, BLK).astype(jnp.float32)
    jitter = jax.random.uniform(third, (NT,), jnp.float32, 0.0, 0.3)
    base = jnp.clip(0.3 * jax.random.normal(first, (NT,), jnp.float32), -1.5, 1.5)
    return base + lift * (20.0 + jitter)


def draw_pairs(key, part):
    first, second, third, fourth = jax.random.split(key, 4)
    rows_index = jnp.arange(NBR, dtype=jnp.int32)
    cols_index = jnp.arange(NBC, dtype=jnp.int32)
    col_pick = jax.random.permutation(first, NBC)
    row_pick = jax.random.permutation(second, NBR)
    base = (cols_index[None, :] == col_pick[rows_index % NBC][:, None]) | (rows_index[:, None] == row_pick[cols_index % NBR][None, :])
    row_tile = ROWS_DEV // BLK
    col_tile = COLS_DEV // BLK
    levels = jax.random.randint(third, (NBR // row_tile, NBC // col_tile), 1, 20)
    level = levels[(rows_index // row_tile)[:, None], (cols_index // col_tile)[None, :]]
    drawn = jax.random.randint(fourth, (NBR, NBC), 0, 32) < level
    return (base | drawn).astype(jnp.int32)


def setup_inputs(seed: int = 0) -> dict:
    splits = jax.random.split(jax.random.key(seed), 5)
    source = draw_source(jax.random.fold_in(splits[4], 71), 0)
    target = draw_target(jax.random.fold_in(splits[4], 71), 0)
    g_init = draw_g_init(jax.random.fold_in(splits[4], 71), 0)
    pairs = draw_pairs(jax.random.fold_in(splits[4], 71), 0)
    return dict(source=source, target=target, g_init=g_init, pairs=pairs)


EPSILON = 0.1
VERY_LOW = -1e30


def block_cost(rows, cols):
    inner = lax.dot_general(rows, cols, (((1,), (1,)), ((), ())), preferred_element_type=jnp.float32)
    left = 0.5 * jnp.sum(jnp.square(rows.astype(jnp.float32)), axis=1)
    right = 0.5 * jnp.sum(jnp.square(cols.astype(jnp.float32)), axis=1)
    return left[:, None] + right[None, :] - inner


def reference(source, target, g_init, pairs):
    log_nt = jnp.log(jnp.float32(NT))
    log_ns = jnp.log(jnp.float32(NS))

    def row_part(index):
        rows = lax.dynamic_slice_in_dim(source, index * BLK, BLK, 0)
        keep = jnp.repeat(lax.dynamic_index_in_dim(pairs, index, 0, keepdims=False) > 0, BLK)
        score = (g_init[None, :] - block_cost(rows, target)) / EPSILON - log_nt
        peak = jnp.max(jnp.where(keep[None, :], score, VERY_LOW), axis=1)
        total = jnp.sum(jnp.where(keep[None, :], jnp.exp(score - peak[:, None]), 0.0), axis=1)
        return -EPSILON * (peak + jnp.log(total))

    f_out = lax.map(row_part, jnp.arange(NBR, dtype=jnp.int32)).reshape(NS)

    def col_step(carry, index):
        peak, total = carry
        rows = lax.dynamic_slice_in_dim(source, index * BLK, BLK, 0)
        values = lax.dynamic_slice_in_dim(f_out, index * BLK, BLK, 0)
        keep = jnp.repeat(lax.dynamic_index_in_dim(pairs, index, 0, keepdims=False) > 0, BLK)
        score = (values[:, None] - block_cost(rows, target)) / EPSILON - log_ns
        block_peak = jnp.max(jnp.where(keep[None, :], score, VERY_LOW), axis=0)
        new_peak = jnp.maximum(peak, block_peak)
        added = jnp.sum(jnp.where(keep[None, :], jnp.exp(score - new_peak[None, :]), 0.0), axis=0)
        total = total * jnp.exp(peak - new_peak) + added
        return (new_peak, total), None

    start = (jnp.full((NT,), VERY_LOW, jnp.float32), jnp.zeros((NT,), jnp.float32))
    (peak, total), _ = lax.scan(col_step, start, jnp.arange(NBR, dtype=jnp.int32))
    g_out = -EPSILON * (peak + jnp.log(total))
    return f_out, g_out
```

```python
import functools
import math

import jax
import jax.numpy as jnp
from jax import lax
from jax.experimental import pallas as pl
from jax.experimental.pallas import tpu as pltpu
from jax.sharding import PartitionSpec as P

EPSILON = 0.1
SCALE = math.log2(math.e) / EPSILON
UNSCALE = EPSILON * math.log(2.0)
VERY_LOW = -1e30
LANES = 128
MESH = pl.DeviceIdType.MESH


def dot_t(left, right):
    return lax.dot_general(
        left, right, (((1,), (1,)), ((), ())), preferred_element_type=jnp.float32
    )


def half_norms(cells):
    wide = cells.astype(jnp.float32)
    square = wide * wide
    high = square.astype(jnp.bfloat16)
    low = (square - high.astype(jnp.float32)).astype(jnp.bfloat16)
    ones = jnp.full((16, cells.shape[1]), 0.5, jnp.bfloat16)
    return (dot_t(ones, high) + dot_t(ones, low))[0:1, :]


def log_sum(parts):
    peak = functools.reduce(jnp.maximum, parts)
    total = functools.reduce(jnp.add, [jnp.exp2(part - peak) for part in parts])
    return peak + jnp.log2(total)


def kernel(
    n_row, n_col, blk, log2_nt, log2_ratio,
    pairs_ref, source_ref, target_ref, g_ref,
    f_ref, g_out_ref,
    sources, targets, scores, peaks, totals, shift, row_parts, col_parts,
    s_send, s_recv, t_send, t_recv, r_send, r_recv, c_send, c_recv,
):
    row, col = lax.axis_index("row"), lax.axis_index("col")
    depth = n_row // 2
    z, core = lax.div(row, 2), lax.rem(row, 2)
    rs, rt = source_ref.shape[0], target_ref.shape[0]
    n_src, n_tgt = sources.shape[0], targets.shape[0]
    width = 2 * rt

    def col_peer(step):
        return lax.rem(col + step, n_col)

    def row_peer(step):
        return lax.rem(row + step, n_row)

    def source_copy(slot, peer):
        return pltpu.make_async_remote_copy(
            src_ref=source_ref,
            dst_ref=sources.at[pl.ds(pl.multiple_of(slot * rs, rs), rs)],
            send_sem=s_send.at[peer], recv_sem=s_recv.at[slot],
            device_id={"col": peer}, device_id_type=MESH,
        )

    def target_copy(shard, way, peer, own=False):
        place = targets.at[pl.ds(pl.multiple_of(shard * rt, rt), rt)]
        return pltpu.make_async_remote_copy(
            src_ref=target_ref if own else place, dst_ref=place,
            send_sem=t_send.at[way, shard], recv_sem=t_recv.at[shard],
            device_id={"row": peer}, device_id_type=MESH,
        )

    def part_copy(parts, send, recv, slot, peer, axis):
        return pltpu.make_async_remote_copy(
            src_ref=parts.at[slot], dst_ref=parts.at[slot],
            send_sem=send.at[peer], recv_sem=recv.at[slot],
            device_id={axis: peer}, device_id_type=MESH,
        )

    sibling = 2 * z + 1 - core
    up, down = row + 2, row - 2

    barrier = pltpu.get_barrier_semaphore()
    for step in range(1, n_row):
        pl.semaphore_signal(
            barrier, inc=1, device_id={"row": row_peer(step)}, device_id_type=MESH
        )
    for step in range(1, n_col):
        pl.semaphore_signal(
            barrier, inc=1, device_id={"col": col_peer(step)}, device_id_type=MESH
        )
    sources[pl.ds(pl.multiple_of(col * rs, rs), rs), :] = source_ref[...]
    targets[pl.ds(pl.multiple_of(row * rt, rt), rt), :] = target_ref[...]
    pl.semaphore_wait(barrier, n_row + n_col - 2)

    @pl.when(z + 1 < depth)
    def _():
        target_copy(row, 0, up, True).start()

    @pl.when(z > 0)
    def _():
        target_copy(row, 1, down, True).start()

    target_copy(row, 2, sibling, True).start()
    for step in range(1, n_col):
        source_copy(col, col_peer(step)).start()

    peaks[...] = jnp.full_like(peaks, VERY_LOW)
    totals[...] = jnp.zeros_like(totals)

    def chunk(level):
        start = pl.multiple_of(level * width, width)
        cells = targets[pl.ds(start, width), :]
        base = (g_ref[:, pl.ds(start, width)] - half_norms(cells)) * SCALE
        block = lax.div(start, blk)

        def rows_step(index, _):
            at = pl.multiple_of(index * LANES, LANES)
            rows = pl.ds(at, LANES)
            kept = pairs_ref[lax.div(at, blk), block].astype(jnp.float32)
            bias = base + (1.0 - kept) * VERY_LOW
            score = dot_t(sources[rows, :], cells) * SCALE + bias
            scores[rows, pl.ds(start, width)] = score
            slices = [score[:, q : q + LANES] for q in range(0, width, LANES)]
            old = peaks[rows, :]
            peak = functools.reduce(jnp.maximum, slices, old)
            total = totals[rows, :] * jnp.exp2(old - peak)
            for part in slices:
                total += jnp.exp2(part - peak)
            peaks[rows, :] = peak
            totals[rows, :] = total
            return 0

        lax.fori_loop(0, n_src // LANES, rows_step, 0)

    for step in range(1, n_col):
        source_copy(col_peer(step), col).wait_recv()
    target_copy(sibling, 2, sibling).wait_recv()
    chunk(z)

    def chain(step, _):
        low, high = z - step, z + step

        @pl.when(low >= 0)
        def _():
            shard = 2 * low + core
            target_copy(shard, 0, down).wait_recv()

            @pl.when(z + 1 < depth)
            def _():
                target_copy(shard, 0, up).start()

            target_copy(shard, 2, sibling).start()

        @pl.when(high < depth)
        def _():
            shard = 2 * high + core
            target_copy(shard, 1, up).wait_recv()

            @pl.when(z > 0)
            def _():
                target_copy(shard, 1, down).start()

            target_copy(shard, 2, sibling).start()

        @pl.when(low >= 0)
        def _():
            target_copy(2 * low + 1 - core, 2, sibling).wait_recv()
            chunk(low)

        @pl.when(high < depth)
        def _():
            target_copy(2 * high + 1 - core, 2, sibling).wait_recv()
            chunk(high)

        return 0

    lax.fori_loop(1, depth, chain, 0)

    for index in range(n_src // LANES):
        rows = slice(index * LANES, (index + 1) * LANES)
        peak_t = peaks[rows, :].T
        total_t = totals[rows, :].T
        peak = jnp.max(peak_t, axis=0, keepdims=True)
        total = jnp.sum(total_t * jnp.exp2(peak_t - peak), axis=0, keepdims=True)
        row_parts[col, index : index + 1, :] = peak + jnp.log2(total)
    for step in range(1, n_col):
        part_copy(row_parts, r_send, r_recv, col, col_peer(step), "col").start()
    for index in range(n_src // LANES):
        cells = sources[index * LANES : (index + 1) * LANES, :]
        f_ref[index : index + 1, :] = half_norms(cells)
    for step in range(1, n_col):
        part_copy(row_parts, r_send, r_recv, col_peer(step), col, "col").wait_recv()
    row_sum = log_sum([row_parts[slot] for slot in range(n_col)])
    f_ref[...] = f_ref[...] + UNSCALE * (log2_nt - row_sum)
    for index in range(n_src // LANES):
        wide = jnp.broadcast_to(row_sum[index : index + 1, :], (LANES, LANES))
        shift[index * LANES : (index + 1) * LANES, :] = wide.T

    group = 4 if n_tgt % (4 * LANES) == 0 else 1
    tall = 64

    def cols_step(index, _):
        start = pl.multiple_of(index * group * LANES, group * LANES)

        def shifted(step):
            rows = pl.ds(pl.multiple_of(step * tall, tall), tall)
            by = shift[rows, :]
            for q in range(group):
                part = scores[rows, pl.ds(start + q * LANES, LANES)] - by
                yield part.reshape(tall // 8, 8, LANES)

        def peak_step(step, carry):
            return tuple(
                jnp.maximum(peak, jnp.max(part, axis=0))
                for peak, part in zip(carry, shifted(step))
            )

        low = jnp.full((8, LANES), VERY_LOW * 2, jnp.float32)
        peak = lax.fori_loop(0, n_src // tall, peak_step, (low,) * group)
        peak = [jnp.max(part, axis=0, keepdims=True) for part in peak]
        wide = [jnp.broadcast_to(part, (8, LANES)) for part in peak]

        def total_step(step, carry):
            return tuple(
                total + jnp.sum(jnp.exp2(part - top[None]), axis=0)
                for total, part, top in zip(carry, shifted(step), wide)
            )

        zero = jnp.zeros((8, LANES), jnp.float32)
        total = lax.fori_loop(0, n_src // tall, total_step, (zero,) * group)
        for q in range(group):
            added = jnp.sum(total[q], axis=0, keepdims=True)
            col_parts[row, pl.ds(index * group + q, 1), :] = peak[q] + jnp.log2(added)
        return 0

    lax.fori_loop(0, n_tgt // (group * LANES), cols_step, 0)

    for step in range(1, n_row):
        part_copy(col_parts, c_send, c_recv, row, row_peer(step), "row").start()
    for step in range(1, n_row):
        part_copy(col_parts, c_send, c_recv, row_peer(step), row, "row").wait_recv()
    col_sum = log_sum([col_parts[slot] for slot in range(n_row)])
    for index in range(n_tgt // LANES):
        lanes = slice(index * LANES, (index + 1) * LANES)
        g_out_ref[index : index + 1, :] = g_ref[:, lanes] - UNSCALE * (
            col_sum[index : index + 1, :] + log2_ratio
        )

    for step in range(1, n_col):
        source_copy(col, col_peer(step)).wait_send()
        part_copy(row_parts, r_send, r_recv, col, col_peer(step), "col").wait_send()
    for step in range(1, n_row):
        part_copy(col_parts, c_send, c_recv, row, row_peer(step), "row").wait_send()
    target_copy(row, 2, sibling).wait_send()

    @pl.when(z + 1 < depth)
    def _():
        target_copy(row, 0, up).wait_send()

    @pl.when(z > 0)
    def _():
        target_copy(row, 1, down).wait_send()

    def drain(step, _):
        low, high = z - step, z + step

        @pl.when(low >= 0)
        def _():
            shard = 2 * low + core
            target_copy(shard, 2, sibling).wait_send()

            @pl.when(z + 1 < depth)
            def _():
                target_copy(shard, 0, up).wait_send()

        @pl.when(high < depth)
        def _():
            shard = 2 * high + core
            target_copy(shard, 2, sibling).wait_send()

            @pl.when(z > 0)
            def _():
                target_copy(shard, 1, down).wait_send()

        return 0

    lax.fori_loop(1, depth, drain, 0)


def local(n_row, n_col, source, target, g_init, pairs):
    rs, dims = source.shape
    rt = target.shape[0]
    n_src, n_tgt = rs * n_col, rt * n_row
    blk = n_src // pairs.shape[0]
    vmem = pl.BlockSpec(memory_space=pltpu.VMEM)
    dma = pltpu.SemaphoreType.DMA
    f_out, g_out = pl.pallas_call(
        functools.partial(
            kernel, n_row, n_col, blk,
            math.log2(n_tgt * n_col), math.log2(n_tgt * n_col) - math.log2(n_src * n_row),
        ),
        out_shape=(
            jax.ShapeDtypeStruct((n_src // LANES, LANES), jnp.float32),
            jax.ShapeDtypeStruct((n_tgt // LANES, LANES), jnp.float32),
        ),
        in_specs=[pl.BlockSpec(memory_space=pltpu.SMEM), vmem, vmem, vmem],
        out_specs=(vmem, vmem),
        scratch_shapes=[
            pltpu.VMEM((n_src, dims), jnp.bfloat16),
            pltpu.VMEM((n_tgt, dims), jnp.bfloat16),
            pltpu.VMEM((n_src, n_tgt), jnp.float32),
            pltpu.VMEM((n_src, LANES), jnp.float32),
            pltpu.VMEM((n_src, LANES), jnp.float32),
            pltpu.VMEM((n_src, LANES), jnp.float32),
            pltpu.VMEM((n_col, n_src // LANES, LANES), jnp.float32),
            pltpu.VMEM((n_row, n_tgt // LANES, LANES), jnp.float32),
            dma((n_col,)), dma((n_col,)),
            dma((3, n_row)), dma((n_row,)),
            dma((n_col,)), dma((n_col,)),
            dma((n_row,)), dma((n_row,)),
        ],
        compiler_params=pltpu.CompilerParams(
            collective_id=0, has_side_effects=True, vmem_limit_bytes=40 * 1024 * 1024
        ),
    )(pairs, source, target, g_init.reshape(1, n_tgt))
    return f_out.reshape(n_src), g_out.reshape(n_tgt)


def solution(mesh):
    return jax.shard_map(
        functools.partial(local, mesh.shape["row"], mesh.shape["col"]),
        mesh=mesh,
        in_specs=(P(("row", "col"), None), P(("col", "row"), None), P("col"), P("row", "col")),
        out_specs=(P("row"), P("col")),
        check_vma=False,
    )
```

```python
import functools
import math

import jax
import jax.numpy as jnp
from jax import lax
from jax.experimental import pallas as pl
from jax.experimental.pallas import tpu as pltpu
from jax.sharding import PartitionSpec as P

EPSILON = 0.1
SCALE = math.log2(math.e) / EPSILON
UNSCALE = EPSILON * math.log(2.0)
VERY_LOW = -1e30
LANES = 128
PIECES = 2
MESH = pl.DeviceIdType.MESH


def dot_t(left, right):
    return lax.dot_general(
        left, right, (((1,), (1,)), ((), ())), preferred_element_type=jnp.float32
    )


def half_norms(cells):
    wide = cells.astype(jnp.float32)
    square = wide * wide
    high = square.astype(jnp.bfloat16)
    low = (square - high.astype(jnp.float32)).astype(jnp.bfloat16)
    ones = jnp.full((16, cells.shape[1]), 0.5, jnp.bfloat16)
    return (dot_t(ones, high) + dot_t(ones, low))[0:1, :]


def log_sum(parts):
    peak = functools.reduce(jnp.maximum, parts)
    total = functools.reduce(jnp.add, [jnp.exp2(part - peak) for part in parts])
    return peak + jnp.log2(total)


def kernel(
    n_row, n_col, blk, log2_nt, log2_ratio,
    pairs_hbm, source_ref, target_ref, g_hbm,
    f_ref, g_out_ref,
    pairs_ref, g_ref, sources, targets, scores, peaks, totals, shift, row_parts, col_parts,
    own_sem, s_send, s_recv, t_send, t_recv, r_send, r_recv, c_send, c_recv,
):
    row, col = lax.axis_index("row"), lax.axis_index("col")
    depth = n_row // 2
    z, core = lax.div(row, 2), lax.rem(row, 2)
    rs, rt = source_ref.shape[0], target_ref.shape[0]
    n_src, n_tgt = sources.shape[0], targets.shape[0]
    width = 2 * rt

    def col_peer(step):
        return lax.rem(col + step, n_col)

    def row_peer(step):
        return lax.rem(row + step, n_row)

    def source_copy(slot, peer):
        return pltpu.make_async_remote_copy(
            src_ref=source_ref,
            dst_ref=sources.at[pl.ds(pl.multiple_of(slot * rs, rs), rs)],
            send_sem=s_send.at[peer], recv_sem=s_recv.at[slot],
            device_id={"col": peer}, device_id_type=MESH,
        )

    size = rt // PIECES

    def target_copy(shard, piece, way, peer, own=False):
        place = targets.at[pl.ds(pl.multiple_of(shard * rt + piece * size, size), size)]
        return pltpu.make_async_remote_copy(
            src_ref=target_ref.at[pl.ds(piece * size, size)] if own else place,
            dst_ref=place,
            send_sem=t_send.at[way, shard, piece], recv_sem=t_recv.at[shard, piece],
            device_id={"row": peer}, device_id_type=MESH,
        )

    def part_copy(parts, send, recv, slot, peer, axis):
        return pltpu.make_async_remote_copy(
            src_ref=parts.at[slot], dst_ref=parts.at[slot],
            send_sem=send.at[peer], recv_sem=recv.at[slot],
            device_id={axis: peer}, device_id_type=MESH,
        )

    sibling = 2 * z + 1 - core
    up, down = row + 2, row - 2

    barrier = pltpu.get_barrier_semaphore()
    for step in range(1, n_row):
        pl.semaphore_signal(
            barrier, inc=1, device_id={"row": row_peer(step)}, device_id_type=MESH
        )
    for step in range(1, n_col):
        pl.semaphore_signal(
            barrier, inc=1, device_id={"col": col_peer(step)}, device_id_type=MESH
        )
    own_copies = [
        pltpu.make_async_copy(src, dst, own_sem.at[index])
        for index, (src, dst) in enumerate((
            (source_ref, sources.at[pl.ds(pl.multiple_of(col * rs, rs), rs)]),
            (target_ref, targets.at[pl.ds(pl.multiple_of(row * rt, rt), rt)]),
            (g_hbm, g_ref),
            (pairs_hbm, pairs_ref),
        ))
    ]
    for copy in own_copies:
        copy.start()
    pl.semaphore_wait(barrier, n_row + n_col - 2)

    for piece in range(PIECES):

        @pl.when(z + 1 < depth)
        def _():
            target_copy(row, piece, 0, up, True).start()

        @pl.when(z > 0)
        def _():
            target_copy(row, piece, 1, down, True).start()

    for step in range(1, n_col):
        source_copy(col, col_peer(step)).start()
    for piece in range(PIECES):
        target_copy(row, piece, 2, sibling, True).start()

    peaks[...] = jnp.full_like(peaks, VERY_LOW)
    totals[...] = jnp.zeros_like(totals)

    def chunk(at):
        start = pl.multiple_of(at * width, width)
        cells = targets[pl.ds(start, width), :]
        base = (g_ref[:, pl.ds(start, width)] - half_norms(cells)) * SCALE
        block = lax.div(start, blk)

        for top in range(0, n_src, blk):
            kept = pairs_ref[top // blk, block].astype(jnp.float32)
            bias = base + (1.0 - kept) * VERY_LOW
            scores[top : top + blk, pl.ds(start, width)] = (
                dot_t(sources[top : top + blk, :], cells) * SCALE + bias
            )

        def rows_step(index, _):
            rows = pl.ds(pl.multiple_of(index * 64, 64), 64)
            slices = [
                scores[rows, pl.ds(start + q, LANES)] for q in range(0, width, LANES)
            ]
            old = peaks[rows, :]
            peak = functools.reduce(jnp.maximum, slices, old)
            total = totals[rows, :] * jnp.exp2(old - peak)
            for part in slices:
                total += jnp.exp2(part - peak)
            peaks[rows, :] = peak
            totals[rows, :] = total
            return 0

        lax.fori_loop(0, n_src // 64, rows_step, 0)

    def forward(step, _):
        low, high = z - step, z + step
        for piece in range(PIECES):

            @pl.when(low >= 0)
            def _():
                shard = 2 * low + core
                target_copy(shard, piece, 0, down).wait_recv()

                @pl.when(z + 1 < depth)
                def _():
                    target_copy(shard, piece, 0, up).start()

                target_copy(shard, piece, 2, sibling).start()

            @pl.when(high < depth)
            def _():
                shard = 2 * high + core
                target_copy(shard, piece, 1, up).wait_recv()

                @pl.when(z > 0)
                def _():
                    target_copy(shard, piece, 1, down).start()

                target_copy(shard, piece, 2, sibling).start()

        return 0

    def level(at):
        for piece in range(PIECES):
            target_copy(2 * at + 1 - core, piece, 2, sibling).wait_recv()
        chunk(at)

    def levels(step, _):
        low, high = z - step, z + step

        @pl.when(low >= 0)
        def _():
            level(low)

        @pl.when(high < depth)
        def _():
            level(high)

        return 0

    lax.fori_loop(1, depth - 1, forward, 0)
    for copy in own_copies:
        copy.wait()
    for step in range(1, n_col):
        source_copy(col_peer(step), col).wait_recv()
    level(z)
    lax.fori_loop(1, depth - 1, levels, 0)
    forward(depth - 1, 0)
    levels(depth - 1, 0)

    for index in range(n_src // LANES):
        rows = slice(index * LANES, (index + 1) * LANES)
        peak_t = peaks[rows, :].T
        total_t = totals[rows, :].T
        peak = jnp.max(peak_t, axis=0, keepdims=True)
        total = jnp.sum(total_t * jnp.exp2(peak_t - peak), axis=0, keepdims=True)
        row_parts[col, index : index + 1, :] = peak + jnp.log2(total)
    for step in range(1, n_col):
        part_copy(row_parts, r_send, r_recv, col, col_peer(step), "col").start()
    for index in range(n_src // LANES):
        cells = sources[index * LANES : (index + 1) * LANES, :]
        f_ref[index : index + 1, :] = half_norms(cells)
    for step in range(1, n_col):
        part_copy(row_parts, r_send, r_recv, col_peer(step), col, "col").wait_recv()
    row_sum = log_sum([row_parts[slot] for slot in range(n_col)])
    f_ref[...] = f_ref[...] + UNSCALE * (log2_nt - row_sum)
    for index in range(n_src // LANES):
        wide = jnp.broadcast_to(row_sum[index : index + 1, :], (LANES, LANES))
        shift[index * LANES : (index + 1) * LANES, :] = wide.T

    group = 4 if n_tgt % (4 * LANES) == 0 else 1
    tall = 64

    def cols_step(index, _):
        start = pl.multiple_of(index * group * LANES, group * LANES)

        def shifted(step):
            rows = pl.ds(pl.multiple_of(step * tall, tall), tall)
            by = shift[rows, :]
            for q in range(group):
                part = scores[rows, pl.ds(start + q * LANES, LANES)] - by
                yield part.reshape(tall // 8, 8, LANES)

        def peak_step(step, carry):
            return tuple(
                jnp.maximum(peak, jnp.max(part, axis=0))
                for peak, part in zip(carry, shifted(step))
            )

        low = jnp.full((8, LANES), VERY_LOW * 2, jnp.float32)
        peak = lax.fori_loop(0, n_src // tall, peak_step, (low,) * group)
        peak = [jnp.max(part, axis=0, keepdims=True) for part in peak]
        wide = [jnp.broadcast_to(part, (8, LANES)) for part in peak]

        def total_step(step, carry):
            return tuple(
                total + jnp.sum(jnp.exp2(part - top[None]), axis=0)
                for total, part, top in zip(carry, shifted(step), wide)
            )

        zero = jnp.zeros((8, LANES), jnp.float32)
        total = lax.fori_loop(0, n_src // tall, total_step, (zero,) * group)
        for q in range(group):
            added = jnp.sum(total[q], axis=0, keepdims=True)
            col_parts[row, pl.ds(index * group + q, 1), :] = peak[q] + jnp.log2(added)
        return 0

    lax.fori_loop(0, n_tgt // (group * LANES), cols_step, 0)

    for step in range(1, n_row):
        part_copy(col_parts, c_send, c_recv, row, row_peer(step), "row").start()
    for step in range(1, n_row):
        part_copy(col_parts, c_send, c_recv, row_peer(step), row, "row").wait_recv()
    col_sum = log_sum([col_parts[slot] for slot in range(n_row)])
    for index in range(n_tgt // LANES):
        lanes = slice(index * LANES, (index + 1) * LANES)
        g_out_ref[index : index + 1, :] = g_ref[:, lanes] - UNSCALE * (
            col_sum[index : index + 1, :] + log2_ratio
        )

    for step in range(1, n_col):
        source_copy(col, col_peer(step)).wait_send()
        part_copy(row_parts, r_send, r_recv, col, col_peer(step), "col").wait_send()
    for step in range(1, n_row):
        part_copy(col_parts, c_send, c_recv, row, row_peer(step), "row").wait_send()
    for piece in range(PIECES):
        target_copy(row, piece, 2, sibling, True).wait_send()

        @pl.when(z + 1 < depth)
        def _():
            target_copy(row, piece, 0, up, True).wait_send()

        @pl.when(z > 0)
        def _():
            target_copy(row, piece, 1, down, True).wait_send()

    def drain(step, _):
        low, high = z - step, z + step
        for piece in range(PIECES):

            @pl.when(low >= 0)
            def _():
                shard = 2 * low + core
                target_copy(shard, piece, 2, sibling).wait_send()

                @pl.when(z + 1 < depth)
                def _():
                    target_copy(shard, piece, 0, up).wait_send()

            @pl.when(high < depth)
            def _():
                shard = 2 * high + core
                target_copy(shard, piece, 2, sibling).wait_send()

                @pl.when(z > 0)
                def _():
                    target_copy(shard, piece, 1, down).wait_send()

        return 0

    lax.fori_loop(1, depth, drain, 0)


def local(n_row, n_col, source, target, g_init, pairs):
    rs, dims = source.shape
    rt = target.shape[0]
    n_src, n_tgt = rs * n_col, rt * n_row
    blk = n_src // pairs.shape[0]
    vmem = pl.BlockSpec(memory_space=pltpu.VMEM)
    dma = pltpu.SemaphoreType.DMA
    f_out, g_out = pl.pallas_call(
        functools.partial(
            kernel, n_row, n_col, blk,
            math.log2(n_tgt * n_col), math.log2(n_tgt * n_col) - math.log2(n_src * n_row),
        ),
        out_shape=(
            jax.ShapeDtypeStruct((n_src // LANES, LANES), jnp.float32),
            jax.ShapeDtypeStruct((n_tgt // LANES, LANES), jnp.float32),
        ),
        in_specs=[pl.BlockSpec(memory_space=pltpu.HBM)] * 4,
        out_specs=(vmem, vmem),
        scratch_shapes=[
            pltpu.SMEM(pairs.shape, jnp.int32),
            pltpu.VMEM((1, n_tgt), jnp.float32),
            pltpu.VMEM((n_src, dims), jnp.bfloat16),
            pltpu.VMEM((n_tgt, dims), jnp.bfloat16),
            pltpu.VMEM((n_src, n_tgt), jnp.float32),
            pltpu.VMEM((n_src, LANES), jnp.float32),
            pltpu.VMEM((n_src, LANES), jnp.float32),
            pltpu.VMEM((n_src, LANES), jnp.float32),
            pltpu.VMEM((n_col, n_src // LANES, LANES), jnp.float32),
            pltpu.VMEM((n_row, n_tgt // LANES, LANES), jnp.float32),
            dma((4,)),
            dma((n_col,)), dma((n_col,)),
            dma((3, n_row, PIECES)), dma((n_row, PIECES)),
            dma((n_col,)), dma((n_col,)),
            dma((n_row,)), dma((n_row,)),
        ],
        compiler_params=pltpu.CompilerParams(
            collective_id=0, has_side_effects=True, vmem_limit_bytes=64 * 1024 * 1024
        ),
    )(pairs, source, target, g_init.reshape(1, n_tgt))
    return f_out.reshape(n_src), g_out.reshape(n_tgt)


def solution(mesh):
    return jax.shard_map(
        functools.partial(local, mesh.shape["row"], mesh.shape["col"]),
        mesh=mesh,
        in_specs=(P(("row", "col"), None), P(("col", "row"), None), P("col"), P("row", "col")),
        out_specs=(P("row"), P("col")),
        check_vma=False,
    )
```

```python
import functools
import math

import jax
import jax.numpy as jnp
from jax import lax
from jax.experimental import pallas as pl
from jax.experimental.pallas import tpu as pltpu
from jax.sharding import PartitionSpec as P

EPSILON = 0.1
SCALE = math.log2(math.e) / EPSILON
UNSCALE = EPSILON * math.log(2.0)
VERY_LOW = -1e30
LANES = 128
PIECES = 2
MESH = pl.DeviceIdType.MESH


def dot_t(left, right):
    return lax.dot_general(
        left, right, (((1,), (1,)), ((), ())), preferred_element_type=jnp.float32
    )


def half_norms(cells):
    wide = cells.astype(jnp.float32)
    square = wide * wide
    high = square.astype(jnp.bfloat16)
    low = (square - high.astype(jnp.float32)).astype(jnp.bfloat16)
    ones = jnp.full((16, cells.shape[1]), 0.5, jnp.bfloat16)
    return (dot_t(ones, high) + dot_t(ones, low))[0:1, :]


def log_sum(parts):
    peak = functools.reduce(jnp.maximum, parts)
    total = functools.reduce(jnp.add, [jnp.exp2(part - peak) for part in parts])
    return peak + jnp.log2(total)


def kernel(
    n_row, n_col, blk, log2_nt, log2_ratio,
    pairs_hbm, source_ref, target_ref, g_hbm,
    f_ref, g_out_ref,
    pairs_ref, g_ref, sources, targets, scores, peaks, totals, shift, row_parts, col_parts,
    own_sem, s_send, s_recv, t_send, t_recv, r_send, r_recv, c_send, c_recv,
):
    row, col = lax.axis_index("row"), lax.axis_index("col")
    depth = n_row // 2
    z, core = lax.div(row, 2), lax.rem(row, 2)
    rs, rt = source_ref.shape[0], target_ref.shape[0]
    n_src, n_tgt = sources.shape[0], targets.shape[0]
    width = 2 * rt

    def col_peer(step):
        return lax.rem(col + step, n_col)

    def row_peer(step):
        return lax.rem(row + step, n_row)

    def source_copy(slot, peer):
        return pltpu.make_async_remote_copy(
            src_ref=source_ref,
            dst_ref=sources.at[pl.ds(pl.multiple_of(slot * rs, rs), rs)],
            send_sem=s_send.at[peer], recv_sem=s_recv.at[slot],
            device_id={"col": peer}, device_id_type=MESH,
        )

    size = rt // PIECES

    def target_copy(shard, piece, way, peer, own=False):
        place = targets.at[pl.ds(pl.multiple_of(shard * rt + piece * size, size), size)]
        return pltpu.make_async_remote_copy(
            src_ref=target_ref.at[pl.ds(piece * size, size)] if own else place,
            dst_ref=place,
            send_sem=t_send.at[way, shard, piece], recv_sem=t_recv.at[shard, piece],
            device_id={"row": peer}, device_id_type=MESH,
        )

    def part_copy(parts, send, recv, slot, peer, axis):
        return pltpu.make_async_remote_copy(
            src_ref=parts.at[slot], dst_ref=parts.at[slot],
            send_sem=send.at[peer], recv_sem=recv.at[slot],
            device_id={axis: peer}, device_id_type=MESH,
        )

    def row_copy(band, slot, peer):
        return pltpu.make_async_remote_copy(
            src_ref=row_parts.at[band, slot], dst_ref=row_parts.at[band, slot],
            send_sem=r_send.at[band, peer], recv_sem=r_recv.at[band, slot],
            device_id={"col": peer}, device_id_type=MESH,
        )

    sibling = 2 * z + 1 - core
    up, down = row + 2, row - 2

    barrier = pltpu.get_barrier_semaphore()
    for step in range(1, n_row):
        pl.semaphore_signal(
            barrier, inc=1, device_id={"row": row_peer(step)}, device_id_type=MESH
        )
    for step in range(1, n_col):
        pl.semaphore_signal(
            barrier, inc=1, device_id={"col": col_peer(step)}, device_id_type=MESH
        )
    own_copies = [
        pltpu.make_async_copy(src, dst, own_sem.at[index])
        for index, (src, dst) in enumerate((
            (source_ref, sources.at[pl.ds(pl.multiple_of(col * rs, rs), rs)]),
            (target_ref, targets.at[pl.ds(pl.multiple_of(row * rt, rt), rt)]),
            (g_hbm, g_ref),
            (pairs_hbm, pairs_ref),
        ))
    ]
    for copy in own_copies:
        copy.start()
    pl.semaphore_wait(barrier, n_row + n_col - 2)

    for piece in range(PIECES):

        @pl.when(z + 1 < depth)
        def _():
            target_copy(row, piece, 0, up, True).start()

        @pl.when(z > 0)
        def _():
            target_copy(row, piece, 1, down, True).start()

    for step in range(1, n_col):
        source_copy(col, col_peer(step)).start()
    for piece in range(PIECES):
        target_copy(row, piece, 2, sibling, True).start()

    peaks[...] = jnp.full_like(peaks, VERY_LOW)
    totals[...] = jnp.zeros_like(totals)

    bands = range(0, n_src, blk)
    per = blk // LANES

    def chunk(at, tops):
        start = pl.multiple_of(at * width, width)
        cells = targets[pl.ds(start, width), :]
        base = (g_ref[:, pl.ds(start, width)] - half_norms(cells)) * SCALE
        block = lax.div(start, blk)

        for top in tops:
            kept = pairs_ref[top // blk, block].astype(jnp.float32)
            bias = base + (1.0 - kept) * VERY_LOW
            scores[top : top + blk, pl.ds(start, width)] = (
                dot_t(sources[top : top + blk, :], cells) * SCALE + bias
            )

        def rows_step(index, _):
            rows = pl.ds(pl.multiple_of(index * 64, 64), 64)
            slices = [
                scores[rows, pl.ds(start + q, LANES)] for q in range(0, width, LANES)
            ]
            old = peaks[rows, :]
            peak = functools.reduce(jnp.maximum, slices, old)
            total = totals[rows, :] * jnp.exp2(old - peak)
            for part in slices:
                total += jnp.exp2(part - peak)
            peaks[rows, :] = peak
            totals[rows, :] = total
            return 0

        lax.fori_loop(tops[0] // 64, (tops[-1] + blk) // 64, rows_step, 0)

    def forward(step, _):
        low, high = z - step, z + step
        for piece in range(PIECES):

            @pl.when(low >= 0)
            def _():
                shard = 2 * low + core
                target_copy(shard, piece, 0, down).wait_recv()

                @pl.when(z + 1 < depth)
                def _():
                    target_copy(shard, piece, 0, up).start()

                target_copy(shard, piece, 2, sibling).start()

            @pl.when(high < depth)
            def _():
                shard = 2 * high + core
                target_copy(shard, piece, 1, up).wait_recv()

                @pl.when(z > 0)
                def _():
                    target_copy(shard, piece, 1, down).start()

                target_copy(shard, piece, 2, sibling).start()

        return 0

    def level(at, tops=bands):
        if tops[0] == 0:
            for piece in range(PIECES):
                target_copy(2 * at + 1 - core, piece, 2, sibling).wait_recv()
        chunk(at, tops)

    def levels(step, _, tops=bands):
        low, high = z - step, z + step

        @pl.when(low >= 0)
        def _():
            level(low, tops)

        @pl.when(high < depth)
        def _():
            level(high, tops)

        return 0

    lax.fori_loop(1, depth - 1, forward, 0)
    for copy in own_copies:
        copy.wait()
    for step in range(1, n_col):
        source_copy(col_peer(step), col).wait_recv()
    level(z)
    lax.fori_loop(1, depth - 1, levels, 0)
    forward(depth - 1, 0)
    for band, top in enumerate(bands):
        levels(depth - 1, 0, range(top, top + blk, blk))
        for index in range(per):
            rows = slice(top + index * LANES, top + (index + 1) * LANES)
            peak_t = peaks[rows, :].T
            total_t = totals[rows, :].T
            peak = jnp.max(peak_t, axis=0, keepdims=True)
            total = jnp.sum(total_t * jnp.exp2(peak_t - peak), axis=0, keepdims=True)
            row_parts[band, col, index : index + 1, :] = peak + jnp.log2(total)
        for step in range(1, n_col):
            row_copy(band, col, col_peer(step)).start()
    for index in range(n_src // LANES):
        cells = sources[index * LANES : (index + 1) * LANES, :]
        f_ref[index : index + 1, :] = half_norms(cells)

    def finish_rows(band):
        for step in range(1, n_col):
            row_copy(band, col_peer(step), col).wait_recv()
        row_sum = log_sum([row_parts[band, slot] for slot in range(n_col)])
        lines = slice(band * per, (band + 1) * per)
        f_ref[lines, :] = f_ref[lines, :] + UNSCALE * (log2_nt - row_sum)
        for index in range(per):
            wide = jnp.broadcast_to(row_sum[index : index + 1, :], (LANES, LANES))
            at = band * blk + index * LANES
            shift[at : at + LANES, :] = wide.T

    group = 4 if n_tgt % (4 * LANES) == 0 else 1
    tall = 256

    def cols_step(band, index, _):
        start = pl.multiple_of(index * group * LANES, group * LANES)

        def shifted(step):
            rows = pl.ds(pl.multiple_of(band * blk + step * tall, tall), tall)
            by = shift[rows, :]
            for q in range(group):
                part = scores[rows, pl.ds(start + q * LANES, LANES)] - by
                yield part.reshape(tall // 8, 8, LANES)

        def peak_step(step, carry):
            return tuple(
                jnp.maximum(peak, jnp.max(part, axis=0))
                for peak, part in zip(carry, shifted(step))
            )

        low = jnp.full((8, LANES), VERY_LOW * 2, jnp.float32)
        peak = lax.fori_loop(0, blk // tall, peak_step, (low,) * group)
        peak = [jnp.max(part, axis=0, keepdims=True) for part in peak]
        wide = [jnp.broadcast_to(part, (8, LANES)) for part in peak]

        def total_step(step, carry):
            return tuple(
                total + jnp.sum(jnp.exp2(part - top[None]), axis=0)
                for total, part, top in zip(carry, shifted(step), wide)
            )

        zero = jnp.zeros((8, LANES), jnp.float32)
        total = lax.fori_loop(0, blk // tall, total_step, (zero,) * group)
        for q in range(group):
            added = jnp.sum(total[q], axis=0, keepdims=True)
            here = peak[q] + jnp.log2(added)
            line = pl.ds(index * group + q, 1)
            if band:
                here = log_sum([col_parts[row, line, :], here])
            col_parts[row, line, :] = here
        return 0

    for band in range(len(bands)):
        finish_rows(band)
        lax.fori_loop(0, n_tgt // (group * LANES), functools.partial(cols_step, band), 0)

    for step in range(1, n_row):
        part_copy(col_parts, c_send, c_recv, row, row_peer(step), "row").start()
    for step in range(1, n_row):
        part_copy(col_parts, c_send, c_recv, row_peer(step), row, "row").wait_recv()
    col_sum = log_sum([col_parts[slot] for slot in range(n_row)])
    for index in range(n_tgt // LANES):
        lanes = slice(index * LANES, (index + 1) * LANES)
        g_out_ref[index : index + 1, :] = g_ref[:, lanes] - UNSCALE * (
            col_sum[index : index + 1, :] + log2_ratio
        )

    for step in range(1, n_col):
        source_copy(col, col_peer(step)).wait_send()
        for band in range(len(bands)):
            row_copy(band, col, col_peer(step)).wait_send()
    for step in range(1, n_row):
        part_copy(col_parts, c_send, c_recv, row, row_peer(step), "row").wait_send()
    for piece in range(PIECES):
        target_copy(row, piece, 2, sibling, True).wait_send()

        @pl.when(z + 1 < depth)
        def _():
            target_copy(row, piece, 0, up, True).wait_send()

        @pl.when(z > 0)
        def _():
            target_copy(row, piece, 1, down, True).wait_send()

    def drain(step, _):
        low, high = z - step, z + step
        for piece in range(PIECES):

            @pl.when(low >= 0)
            def _():
                shard = 2 * low + core
                target_copy(shard, piece, 2, sibling).wait_send()

                @pl.when(z + 1 < depth)
                def _():
                    target_copy(shard, piece, 0, up).wait_send()

            @pl.when(high < depth)
            def _():
                shard = 2 * high + core
                target_copy(shard, piece, 2, sibling).wait_send()

                @pl.when(z > 0)
                def _():
                    target_copy(shard, piece, 1, down).wait_send()

        return 0

    lax.fori_loop(1, depth, drain, 0)


def local(n_row, n_col, source, target, g_init, pairs):
    rs, dims = source.shape
    rt = target.shape[0]
    n_src, n_tgt = rs * n_col, rt * n_row
    blk = n_src // pairs.shape[0]
    vmem = pl.BlockSpec(memory_space=pltpu.VMEM)
    dma = pltpu.SemaphoreType.DMA
    f_out, g_out = pl.pallas_call(
        functools.partial(
            kernel, n_row, n_col, blk,
            math.log2(n_tgt * n_col), math.log2(n_tgt * n_col) - math.log2(n_src * n_row),
        ),
        out_shape=(
            jax.ShapeDtypeStruct((n_src // LANES, LANES), jnp.float32),
            jax.ShapeDtypeStruct((n_tgt // LANES, LANES), jnp.float32),
        ),
        in_specs=[pl.BlockSpec(memory_space=pltpu.HBM)] * 4,
        out_specs=(vmem, vmem),
        scratch_shapes=[
            pltpu.SMEM(pairs.shape, jnp.int32),
            pltpu.VMEM((1, n_tgt), jnp.float32),
            pltpu.VMEM((n_src, dims), jnp.bfloat16),
            pltpu.VMEM((n_tgt, dims), jnp.bfloat16),
            pltpu.VMEM((n_src, n_tgt), jnp.float32),
            pltpu.VMEM((n_src, LANES), jnp.float32),
            pltpu.VMEM((n_src, LANES), jnp.float32),
            pltpu.VMEM((n_src, LANES), jnp.float32),
            pltpu.VMEM((n_src // blk, n_col, blk // LANES, LANES), jnp.float32),
            pltpu.VMEM((n_row, n_tgt // LANES, LANES), jnp.float32),
            dma((4,)),
            dma((n_col,)), dma((n_col,)),
            dma((3, n_row, PIECES)), dma((n_row, PIECES)),
            dma((n_src // blk, n_col)), dma((n_src // blk, n_col)),
            dma((n_row,)), dma((n_row,)),
        ],
        compiler_params=pltpu.CompilerParams(
            collective_id=0, has_side_effects=True, vmem_limit_bytes=64 * 1024 * 1024
        ),
    )(pairs, source, target, g_init.reshape(1, n_tgt))
    return f_out.reshape(n_src), g_out.reshape(n_tgt)


def solution(mesh):
    return jax.shard_map(
        functools.partial(local, mesh.shape["row"], mesh.shape["col"]),
        mesh=mesh,
        in_specs=(P(("row", "col"), None), P(("col", "row"), None), P("col"), P("row", "col")),
        out_specs=(P("row"), P("col")),
        check_vma=False,
    )
```

```python
import functools
import math

import jax
import jax.numpy as jnp
from jax import lax
from jax.experimental import pallas as pl
from jax.experimental.pallas import tpu as pltpu
from jax.sharding import PartitionSpec as P

EPSILON = 0.1
SCALE = math.log2(math.e) / EPSILON
UNSCALE = EPSILON * math.log(2.0)
VERY_LOW = -1e30
LANES = 128
PIECES = 2
MESH = pl.DeviceIdType.MESH


def dot_t(left, right):
    return lax.dot_general(
        left, right, (((1,), (1,)), ((), ())), preferred_element_type=jnp.float32
    )


def half_norms(cells):
    wide = cells.astype(jnp.float32)
    square = wide * wide
    high = square.astype(jnp.bfloat16)
    low = (square - high.astype(jnp.float32)).astype(jnp.bfloat16)
    ones = jnp.full((16, cells.shape[1]), 0.5, jnp.bfloat16)
    return (dot_t(ones, high) + dot_t(ones, low))[0:1, :]


def log_sum(parts):
    peak = functools.reduce(jnp.maximum, parts)
    total = functools.reduce(jnp.add, [jnp.exp2(part - peak) for part in parts])
    return peak + jnp.log2(total)


def kernel(
    n_row, n_col, blk, log2_nt, log2_ratio,
    pairs_hbm, source_ref, target_ref, g_hbm,
    f_ref, g_out_ref,
    pairs_ref, g_ref, sources, targets, scores, peaks, totals, shift, row_parts, col_parts,
    own_sem, s_send, s_recv, t_send, t_recv, r_send, r_recv, c_send, c_recv,
):
    row, col = lax.axis_index("row"), lax.axis_index("col")
    depth = n_row // 2
    z, core = lax.div(row, 2), lax.rem(row, 2)
    rs, rt = source_ref.shape[0], target_ref.shape[0]
    n_src, n_tgt = sources.shape[0], targets.shape[0]
    width = 2 * rt

    def col_peer(step):
        return lax.rem(col + step, n_col)

    def row_peer(step):
        return lax.rem(row + step, n_row)

    def source_copy(slot, peer):
        return pltpu.make_async_remote_copy(
            src_ref=source_ref,
            dst_ref=sources.at[pl.ds(pl.multiple_of(slot * rs, rs), rs)],
            send_sem=s_send.at[peer], recv_sem=s_recv.at[slot],
            device_id={"col": peer}, device_id_type=MESH,
        )

    size = rt // PIECES

    def target_copy(shard, piece, way, peer, own=False):
        place = targets.at[pl.ds(pl.multiple_of(shard * rt + piece * size, size), size)]
        return pltpu.make_async_remote_copy(
            src_ref=target_ref.at[pl.ds(piece * size, size)] if own else place,
            dst_ref=place,
            send_sem=t_send.at[way, shard, piece], recv_sem=t_recv.at[shard, piece],
            device_id={"row": peer}, device_id_type=MESH,
        )

    def part_copy(parts, send, recv, slot, peer, axis):
        return pltpu.make_async_remote_copy(
            src_ref=parts.at[slot], dst_ref=parts.at[slot],
            send_sem=send.at[peer], recv_sem=recv.at[slot],
            device_id={axis: peer}, device_id_type=MESH,
        )

    def row_copy(band, slot, peer):
        return pltpu.make_async_remote_copy(
            src_ref=row_parts.at[band, slot], dst_ref=row_parts.at[band, slot],
            send_sem=r_send.at[band, peer], recv_sem=r_recv.at[band, slot],
            device_id={"col": peer}, device_id_type=MESH,
        )

    sibling = 2 * z + 1 - core
    up, down = row + 2, row - 2

    barrier = pltpu.get_barrier_semaphore()
    for step in range(1, n_row):
        pl.semaphore_signal(
            barrier, inc=1, device_id={"row": row_peer(step)}, device_id_type=MESH
        )
    for step in range(1, n_col):
        pl.semaphore_signal(
            barrier, inc=1, device_id={"col": col_peer(step)}, device_id_type=MESH
        )
    own_copies = [
        pltpu.make_async_copy(src, dst, own_sem.at[index])
        for index, (src, dst) in enumerate((
            (source_ref, sources.at[pl.ds(pl.multiple_of(col * rs, rs), rs)]),
            (target_ref, targets.at[pl.ds(pl.multiple_of(row * rt, rt), rt)]),
            (g_hbm, g_ref),
            (pairs_hbm, pairs_ref),
        ))
    ]
    for copy in own_copies:
        copy.start()
    pl.semaphore_wait(barrier, n_row + n_col - 2)

    for piece in range(PIECES):

        @pl.when(z + 1 < depth)
        def _():
            target_copy(row, piece, 0, up, True).start()

        @pl.when(z > 0)
        def _():
            target_copy(row, piece, 1, down, True).start()

    for step in range(1, n_col):
        source_copy(col, col_peer(step)).start()
    for piece in range(PIECES):
        target_copy(row, piece, 2, sibling, True).start()

    peaks[...] = jnp.full_like(peaks, VERY_LOW)
    totals[...] = jnp.zeros_like(totals)

    bands = range(0, n_src, blk)
    per = blk // LANES

    def chunk(at, tops):
        start = pl.multiple_of(at * width, width)
        cells = targets[pl.ds(start, width), :]
        base = (g_ref[:, pl.ds(start, width)] - half_norms(cells)) * SCALE
        block = lax.div(start, blk)

        for top in tops:
            kept = pairs_ref[top // blk, block].astype(jnp.float32)
            bias = base + (1.0 - kept) * VERY_LOW
            scores[top : top + blk, pl.ds(start, width)] = (
                dot_t(sources[top : top + blk, :], cells) * SCALE + bias
            )

        def rows_step(index, _):
            rows = pl.ds(pl.multiple_of(index * LANES, LANES), LANES)
            slices = [
                scores[rows, pl.ds(start + q, LANES)] for q in range(0, width, LANES)
            ]
            old = peaks[rows, :]
            peak = functools.reduce(jnp.maximum, slices, old)
            total = totals[rows, :] * jnp.exp2(old - peak)
            for part in slices:
                total += jnp.exp2(part - peak)
            peaks[rows, :] = peak
            totals[rows, :] = total
            return 0

        lax.fori_loop(tops[0] // LANES, (tops[-1] + blk) // LANES, rows_step, 0)

    def forward(step, _):
        low, high = z - step, z + step
        for piece in range(PIECES):

            @pl.when(low >= 0)
            def _():
                shard = 2 * low + core
                target_copy(shard, piece, 0, down).wait_recv()

                @pl.when(z + 1 < depth)
                def _():
                    target_copy(shard, piece, 0, up).start()

                target_copy(shard, piece, 2, sibling).start()

            @pl.when(high < depth)
            def _():
                shard = 2 * high + core
                target_copy(shard, piece, 1, up).wait_recv()

                @pl.when(z > 0)
                def _():
                    target_copy(shard, piece, 1, down).start()

                target_copy(shard, piece, 2, sibling).start()

        return 0

    def level(at, tops=bands):
        if tops[0] == 0:
            for piece in range(PIECES):
                target_copy(2 * at + 1 - core, piece, 2, sibling).wait_recv()
        chunk(at, tops)

    def levels(step, _, tops=bands):
        low, high = z - step, z + step

        @pl.when(low >= 0)
        def _():
            level(low, tops)

        @pl.when(high < depth)
        def _():
            level(high, tops)

        return 0

    lax.fori_loop(1, depth - 1, forward, 0)
    for copy in own_copies:
        copy.wait()
    for step in range(1, n_col):
        source_copy(col_peer(step), col).wait_recv()
    level(z)
    lax.fori_loop(1, depth - 1, levels, 0)
    forward(depth - 1, 0)
    for band, top in enumerate(bands):
        levels(depth - 1, 0, range(top, top + blk, blk))
        for index in range(per):
            rows = slice(top + index * LANES, top + (index + 1) * LANES)
            peak_t = peaks[rows, :].T
            total_t = totals[rows, :].T
            peak = jnp.max(peak_t, axis=0, keepdims=True)
            total = jnp.sum(total_t * jnp.exp2(peak_t - peak), axis=0, keepdims=True)
            row_parts[band, col, index : index + 1, :] = peak + jnp.log2(total)
        for step in range(1, n_col):
            row_copy(band, col, col_peer(step)).start()
    for index in range(n_src // LANES):
        cells = sources[index * LANES : (index + 1) * LANES, :]
        f_ref[index : index + 1, :] = half_norms(cells)

    def finish_rows(band):
        for step in range(1, n_col):
            row_copy(band, col_peer(step), col).wait_recv()
        row_sum = log_sum([row_parts[band, slot] for slot in range(n_col)])
        lines = slice(band * per, (band + 1) * per)
        f_ref[lines, :] = f_ref[lines, :] + UNSCALE * (log2_nt - row_sum)
        for index in range(per):
            wide = jnp.broadcast_to(row_sum[index : index + 1, :], (LANES, LANES))
            at = band * blk + index * LANES
            shift[at : at + LANES, :] = wide.T

    group = 4 if n_tgt % (4 * LANES) == 0 else 1
    tall = blk

    def cols_step(band, index, _):
        start = pl.multiple_of(index * group * LANES, group * LANES)

        def shifted(step):
            rows = pl.ds(pl.multiple_of(band * blk + step * tall, tall), tall)
            by = shift[rows, :]
            for q in range(group):
                part = scores[rows, pl.ds(start + q * LANES, LANES)] - by
                yield part.reshape(tall // 8, 8, LANES)

        def peak_step(step, carry):
            return tuple(
                jnp.maximum(peak, jnp.max(part, axis=0))
                for peak, part in zip(carry, shifted(step))
            )

        low = jnp.full((8, LANES), VERY_LOW * 2, jnp.float32)
        peak = lax.fori_loop(0, blk // tall, peak_step, (low,) * group)
        peak = [jnp.max(part, axis=0, keepdims=True) for part in peak]
        wide = [jnp.broadcast_to(part, (8, LANES)) for part in peak]

        def total_step(step, carry):
            return tuple(
                total + jnp.sum(jnp.exp2(part - top[None]), axis=0)
                for total, part, top in zip(carry, shifted(step), wide)
            )

        zero = jnp.zeros((8, LANES), jnp.float32)
        total = lax.fori_loop(0, blk // tall, total_step, (zero,) * group)
        for q in range(group):
            added = jnp.sum(total[q], axis=0, keepdims=True)
            here = peak[q] + jnp.log2(added)
            line = pl.ds(index * group + q, 1)
            if band:
                here = log_sum([col_parts[row, line, :], here])
            col_parts[row, line, :] = here
        return 0

    for band in range(len(bands)):
        finish_rows(band)
        lax.fori_loop(0, n_tgt // (group * LANES), functools.partial(cols_step, band), 0)

    for step in range(1, n_row):
        part_copy(col_parts, c_send, c_recv, row, row_peer(step), "row").start()
    for step in range(1, n_row):
        part_copy(col_parts, c_send, c_recv, row_peer(step), row, "row").wait_recv()
    col_sum = log_sum([col_parts[slot] for slot in range(n_row)])
    for index in range(n_tgt // LANES):
        lanes = slice(index * LANES, (index + 1) * LANES)
        g_out_ref[index : index + 1, :] = g_ref[:, lanes] - UNSCALE * (
            col_sum[index : index + 1, :] + log2_ratio
        )

    for step in range(1, n_col):
        source_copy(col, col_peer(step)).wait_send()
        for band in range(len(bands)):
            row_copy(band, col, col_peer(step)).wait_send()
    for step in range(1, n_row):
        part_copy(col_parts, c_send, c_recv, row, row_peer(step), "row").wait_send()
    for piece in range(PIECES):
        target_copy(row, piece, 2, sibling, True).wait_send()

        @pl.when(z + 1 < depth)
        def _():
            target_copy(row, piece, 0, up, True).wait_send()

        @pl.when(z > 0)
        def _():
            target_copy(row, piece, 1, down, True).wait_send()

    def drain(step, _):
        low, high = z - step, z + step
        for piece in range(PIECES):

            @pl.when(low >= 0)
            def _():
                shard = 2 * low + core
                target_copy(shard, piece, 2, sibling).wait_send()

                @pl.when(z + 1 < depth)
                def _():
                    target_copy(shard, piece, 0, up).wait_send()

            @pl.when(high < depth)
            def _():
                shard = 2 * high + core
                target_copy(shard, piece, 2, sibling).wait_send()

                @pl.when(z > 0)
                def _():
                    target_copy(shard, piece, 1, down).wait_send()

        return 0

    lax.fori_loop(1, depth, drain, 0)


def local(n_row, n_col, source, target, g_init, pairs):
    rs, dims = source.shape
    rt = target.shape[0]
    n_src, n_tgt = rs * n_col, rt * n_row
    blk = n_src // pairs.shape[0]
    vmem = pl.BlockSpec(memory_space=pltpu.VMEM)
    dma = pltpu.SemaphoreType.DMA
    f_out, g_out = pl.pallas_call(
        functools.partial(
            kernel, n_row, n_col, blk,
            math.log2(n_tgt * n_col), math.log2(n_tgt * n_col) - math.log2(n_src * n_row),
        ),
        out_shape=(
            jax.ShapeDtypeStruct((n_src // LANES, LANES), jnp.float32),
            jax.ShapeDtypeStruct((n_tgt // LANES, LANES), jnp.float32),
        ),
        in_specs=[pl.BlockSpec(memory_space=pltpu.HBM)] * 4,
        out_specs=(vmem, vmem),
        scratch_shapes=[
            pltpu.SMEM(pairs.shape, jnp.int32),
            pltpu.VMEM((1, n_tgt), jnp.float32),
            pltpu.VMEM((n_src, dims), jnp.bfloat16),
            pltpu.VMEM((n_tgt, dims), jnp.bfloat16),
            pltpu.VMEM((n_src, n_tgt), jnp.float32),
            pltpu.VMEM((n_src, LANES), jnp.float32),
            pltpu.VMEM((n_src, LANES), jnp.float32),
            pltpu.VMEM((n_src, LANES), jnp.float32),
            pltpu.VMEM((n_src // blk, n_col, blk // LANES, LANES), jnp.float32),
            pltpu.VMEM((n_row, n_tgt // LANES, LANES), jnp.float32),
            dma((4,)),
            dma((n_col,)), dma((n_col,)),
            dma((3, n_row, PIECES)), dma((n_row, PIECES)),
            dma((n_src // blk, n_col)), dma((n_src // blk, n_col)),
            dma((n_row,)), dma((n_row,)),
        ],
        compiler_params=pltpu.CompilerParams(
            collective_id=0, has_side_effects=True, vmem_limit_bytes=64 * 1024 * 1024
        ),
    )(pairs, source, target, g_init.reshape(1, n_tgt))
    return f_out.reshape(n_src), g_out.reshape(n_tgt)


def solution(mesh):
    return jax.shard_map(
        functools.partial(local, mesh.shape["row"], mesh.shape["col"]),
        mesh=mesh,
        in_specs=(P(("row", "col"), None), P(("col", "row"), None), P("col"), P("row", "col")),
        out_specs=(P("row"), P("col")),
        check_vma=False,
    )
```
